32 devices in a mesh: blocks: 2 (over x), mode: 16 (over z, y, core).
Axes of the slice: x: 2, y: 2, z: 4, core: 2. Of those that a mesh axis runs over, the one named last changes fastest.
Arguments:
- right_side: float32 [2, 8, 1024, 1024], P(None, 'blocks', 'mode'), parts along dimension 1, may hold values from -6 to 6
- classes: int32 [8, 1024, 1024], P('blocks', 'mode'), parts along dimension 0, may hold values from 0 to 7
- noise_table: float32 [8], replicated, may hold values from 0.05 to 1
- kernel_first: bfloat16 [1024, 1024], replicated, may hold values from -1 to 3, as said below
- kernel_second: bfloat16 [1024, 1024], replicated, may hold values from -1 to 3, as said below
- basis_first: bfloat16 [1024, 1024], replicated, may hold values from -1 to 2, as said below
- basis_second: bfloat16 [1024, 1024], replicated, may hold values from -1 to 2, as said below
- eigen_first: float32 [1024], replicated, may hold values from 0.5 to 4
- eigen_second: float32 [1024], P('mode'), may hold values from 0.5 to 4
Outputs:
- solution_field: float32 [2, 8, 1024, 1024], P(None, 'blocks', 'mode'), parts along dimension 1
- residual: float32 [2, 8, 1024, 1024], P(None, 'blocks', 'mode'), parts along dimension 1
The draws below stay inside these ranges and needn't reach their ends.
There are 2 independent parts, one for each index of `blocks`. The reference program is written for one: setup_inputs(seed, part) draws one part's arguments, and reference() takes and returns one part's arrays. A program takes and returns all parts, laid end to end along the dimension named above; an argument that names none is the same for every part. Nothing has to cross between parts.
Inputs may be any that keep to these rules, and one draw needn't show every extreme that they name: `kernel_first`: symmetric positive definite. `kernel_second`: symmetric positive definite. `basis_first`: nonsingular. `basis_second`: nonsingular.
All inputs are finite; a program needn't handle non-finite values.
Results may differ from the reference program's by a relative error of at most 0.0003.
Values sent between devices are 32-bit elements; how exact they have to be, the bound alone decides.
A program may use at most 128 MiB of HBM per device.

```python
import math
import jax
import jax.numpy as jnp
from jax import lax

N1 = 1024
N2 = 1024
PLANES = 4
SAMPLES = 2
NCLASS = 8
ITERS = 2


def make_kernel(key, width):
    gauss = jax.random.normal(key, (width, width), jnp.float32) / jnp.sqrt(jnp.float32(width))
    product = jnp.dot(gauss, gauss.T, precision=lax.Precision.HIGHEST)
    return (product + 0.5 * jnp.eye(width, dtype=jnp.float32)).astype(jnp.bfloat16)


def make_basis(key, width):
    gauss = jax.random.normal(key, (width, width), jnp.float32) / jnp.sqrt(jnp.float32(width))
    return (jnp.eye(width, dtype=jnp.float32) + 0.3 * gauss).astype(jnp.bfloat16)


def draw_kernel_first(key, part):
    return make_kernel(jax.random.fold_in(key, 11), N1)


def draw_kernel_second(key, part):
    return make_kernel(jax.random.fold_in(key, 12), N2)


def draw_basis_first(key, part):
    return make_basis(jax.random.fold_in(key, 13), N1)


def draw_basis_second(key, part):
    return make_basis(jax.random.fold_in(key, 14), N2)


def with_ends(drawn, stream_key, smallest, top_value):
    spot = [jax.random.randint(jax.random.fold_in(stream_key, axis), (), 0, length) for axis, length in enumerate(drawn.shape)]
    main_axis = drawn.shape.index(max(drawn.shape))
    neighbour = spot[:main_axis] + [(spot[main_axis] + 1) % drawn.shape[main_axis]] + spot[main_axis + 1:]
    return drawn.at[tuple(spot)].set(smallest).at[tuple(neighbour)].set(top_value)


def steps_of(key, shape, cuts, least, high):
    def one(position, blocks):
        draws = jax.random.uniform(jax.random.fold_in(jax.random.fold_in(key, 6), position), (blocks,), jnp.float32, least / len(cuts), high / len(cuts))
        return jnp.repeat(jnp.exp(draws), shape[position] // blocks).reshape((-1,) + (1,) * (len(shape) - position - 1))

    loudness = one(*cuts[0])
    for cut in cuts[1:]:
        loudness = loudness * one(*cut)
    return loudness


def bell_draw(key, shape, scale, most, split=(), kind=jnp.bfloat16):
    result = jax.random.normal(key, shape, jnp.float32) * scale
    if len(split) > 0:
        result = steps_of(key, shape, split, -0.22, 0.18) * result
    return jnp.clip(result, min=-most, max=most).astype(kind)


def setup_inputs(seed: int = 0, part: int = 0) -> dict:
    streams_of = jax.random.split(jax.random.key(seed), 10)
    own_keys = jax.random.split(jax.random.fold_in(streams_of[9], part), 10)
    right_side = bell_draw(own_keys[0], (SAMPLES, PLANES, N1, N2), 1.0, 6.0, ((2, 16),), jnp.float32)
    classes = with_ends(jax.random.randint(own_keys[1], (PLANES, N1, N2), 0, NCLASS), jax.random.fold_in(own_keys[1], 1), 0, NCLASS - 1).astype(jnp.int32)
    noise_table = jnp.clip(jnp.exp(jax.random.uniform(streams_of[2], (NCLASS,), jnp.float32, math.log(0.05), math.log(1.0))), 0.05, 1.0)
    kernel_first = draw_kernel_first(jax.random.fold_in(streams_of[9], 71), part)
    kernel_second = draw_kernel_second(jax.random.fold_in(streams_of[9], 71), part)
    basis_first = draw_basis_first(jax.random.fold_in(streams_of[9], 71), part)
    basis_second = draw_basis_second(jax.random.fold_in(streams_of[9], 71), part)
    eigen_first = jnp.clip(jnp.exp(jax.random.uniform(streams_of[7], (N1,), jnp.float32, math.log(0.5), math.log(4.0))), 0.5, 4.0)
    eigen_second = jnp.clip(jnp.exp(math.log(4.0) - 2.0794415 * jax.random.uniform(streams_of[8], (N2,), jnp.float32) ** steps_of(streams_of[8], (N2,), ((0, 16),), -0.2, 0.2)), 0.5, 4.0)
    return {"right_side": right_side, "classes": classes, "noise_table": noise_table, "kernel_first": kernel_first, "kernel_second": kernel_second, "basis_first": basis_first, "basis_second": basis_second, "eigen_first": eigen_first, "eigen_second": eigen_second}


def first(matrix, field):
    return jnp.einsum('ik,spkj->spij', matrix.astype(jnp.float32), field, precision=lax.Precision.HIGHEST)


def second(matrix, field):
    return jnp.einsum('jk,spik->spij', matrix.astype(jnp.float32), field, precision=lax.Precision.HIGHEST)


def reference(right_side, classes, noise_table, kernel_first, kernel_second, basis_first, basis_second, eigen_first, eigen_second):
    noise = noise_table[classes]
    mean_noise = jnp.mean(noise_table)
    weights = 1.0 / (eigen_first[:, None] * eigen_second[None, :] + mean_noise)

    def operate(field):
        return first(kernel_first, second(kernel_second, field)) + noise[None] * field

    def precond(field):
        inner = first(basis_first.T, second(basis_second.T, field)) * weights
        return first(basis_first, second(basis_second, inner))

    solution_field = jnp.zeros_like(right_side)
    residual = right_side
    z_field = precond(residual)
    direction = z_field
    gamma = jnp.sum(residual * z_field)
    for step in range(ITERS):
        image = operate(direction)
        alpha = gamma / jnp.sum(direction * image)
        solution_field = solution_field + alpha * direction
        residual = residual - alpha * image
        if step + 1 < ITERS:
            z_field = precond(residual)
            gamma_new = jnp.sum(residual * z_field)
            direction = z_field + (gamma_new / gamma) * direction
            gamma = gamma_new
    return solution_field, residual
```

```python
import jax
import jax.numpy as jnp
from jax import lax
from jax.sharding import PartitionSpec as P

ITERS = 2


def split(field):
    high = lax.reduce_precision(field, 8, 7)
    return high.astype(jnp.bfloat16), (field - high).astype(jnp.bfloat16)


def dot(left, right, dims):
    return lax.dot_general(left, right, (dims, ((), ())), preferred_element_type=jnp.float32)


def on_first(matrix, field, transposed=False):
    dims = ((0 if transposed else 1,), (0,))
    high, low = split(field)
    return dot(matrix, high, dims) + dot(matrix, low, dims)


def on_second(matrix, field, transposed=False):
    dims = ((1,), (0 if transposed else 1,))
    high, low = split(field)
    return dot(high, matrix, dims) + dot(low, matrix, dims)


def body(
    right_side,
    classes,
    noise_table,
    kernel_first,
    kernel_second,
    basis_first,
    basis_second,
    eigen_first,
    eigen_second,
):
    devices = lax.axis_size("mode")
    samples, planes, rows, width = right_side.shape
    height = eigen_first.shape[0]
    fields = samples * planes
    share = devices // fields
    cols = width // share
    near = [[f * share + c for c in range(share)] for f in range(fields)]
    twins = [
        [(p * samples + s) * share + c for s in range(samples)]
        for p in range(planes)
        for c in range(share)
    ]
    me = lax.axis_index("mode")
    mine = lax.rem(me, share)

    def to_all(blocks):
        return lax.all_to_all(blocks, "mode", split_axis=0, concat_axis=0, tiled=True)

    def to_rows(field):
        return lax.all_to_all(
            field, "mode", split_axis=0, concat_axis=1, axis_index_groups=near, tiled=True
        )

    def to_columns(field):
        return lax.all_to_all(
            field, "mode", split_axis=1, concat_axis=0, axis_index_groups=near, tiled=True
        )

    def give_back(field):
        got = to_all(field.reshape(devices, rows, cols))
        got = got.reshape(planes, samples, share, rows, cols)
        return got.transpose(1, 0, 3, 2, 4).reshape(right_side.shape)

    level = jnp.take(noise_table, 0) * jnp.ones(classes.shape, jnp.float32)
    for index in range(1, noise_table.shape[0]):
        level = jnp.where(classes == index, noise_table[index], level)
    mean_noise = jnp.mean(noise_table)

    part = cols // samples
    outgoing = level.reshape(planes, rows, share, samples, part).transpose(0, 3, 2, 1, 4)
    quarter = to_all(outgoing.reshape(devices, rows, part)).reshape(height, part)
    noise = lax.all_gather(quarter, "mode", axis=1, axis_index_groups=twins, tiled=True)

    all_second = lax.all_gather(eigen_second, "mode", tiled=True)
    weights = 1.0 / (eigen_first[:, None] * all_second[None, :] + mean_noise)
    row_count = height // share
    row_weights = lax.dynamic_slice_in_dim(weights, mine * row_count, row_count, 0)
    col_weights = lax.dynamic_slice_in_dim(weights, mine * cols, cols, 1)

    turned = on_second(basis_second, right_side.reshape(-1, width), True)
    outgoing = turned.reshape(samples, planes, rows, share, cols).transpose(1, 0, 3, 2, 4)
    incoming = to_all(outgoing.reshape(devices, rows, cols)).reshape(height, cols)

    spectrum = on_first(basis_first, incoming, True)
    weighted = col_weights * spectrum
    gamma_part = jnp.sum(spectrum * weighted)
    spectrum_rows = to_rows(spectrum)
    direction_rows = on_second(basis_second, to_rows(on_first(basis_first, weighted)))
    direction = to_columns(direction_rows)
    image = on_first(kernel_first, to_columns(on_second(kernel_second, direction_rows)))
    image = image + noise * direction
    curve_part = jnp.sum(direction * image)
    gamma, curvature = lax.psum(jnp.stack([gamma_part, curve_part]), "mode")
    alpha = gamma / curvature
    change = on_second(basis_second, to_rows(on_first(basis_first, image, True)), True)
    spectrum_rows = spectrum_rows - alpha * change
    weighted = row_weights * spectrum_rows
    gamma_part = jnp.sum(spectrum_rows * weighted)
    later_rows = to_columns(on_second(basis_second, weighted))
    later = on_first(basis_first, later_rows)
    later_image = on_first(kernel_first, to_columns(on_second(kernel_second, to_rows(later))))
    later_image = later_image + noise * later
    parts = jnp.stack([gamma_part, jnp.sum(later * later_image), jnp.sum(later * image)])
    gamma_new, own, cross = lax.psum(parts, "mode")
    ratio = gamma_new / gamma
    step = gamma_new / (own + ratio * (2.0 * cross + ratio * curvature))
    before = alpha + step * ratio
    solution_field = give_back(before * direction + step * later)
    applied = give_back(before * image + step * later_image)
    return solution_field, right_side - applied


def solution(mesh):
    in_specs = (
        P(None, "blocks", "mode", None),
        P("blocks", "mode", None),
        P(),
        P(),
        P(),
        P(),
        P(),
        P(),
        P("mode"),
    )
    out_specs = (P(None, "blocks", "mode", None), P(None, "blocks", "mode", None))
    return jax.shard_map(body, mesh=mesh, in_specs=in_specs, out_specs=out_specs, check_vma=False)
```

```python
import jax
import jax.numpy as jnp
from jax import lax
from jax.experimental import pallas as pl
from jax.experimental.pallas import tpu as pltpu
from jax.sharding import PartitionSpec as P

ITERS = 2


def split(field):
    high = lax.reduce_precision(field, 8, 7)
    return high.astype(jnp.bfloat16), (field - high).astype(jnp.bfloat16)


def dot(left, right, dims):
    return lax.dot_general(left, right, (dims, ((), ())), preferred_element_type=jnp.float32)


def on_first(matrix, field, transposed=False):
    dims = ((0 if transposed else 1,), (0,))
    high, low = split(field)
    return dot(matrix, high, dims) + dot(matrix, low, dims)


def on_second(matrix, field, transposed=False):
    dims = ((1,), (0 if transposed else 1,))
    high, low = split(field)
    return dot(high, matrix, dims) + dot(low, matrix, dims)


def general_body(
    right_side,
    classes,
    noise_table,
    kernel_first,
    kernel_second,
    basis_first,
    basis_second,
    eigen_first,
    eigen_second,
):
    devices = lax.axis_size("mode")
    samples, planes, rows, width = right_side.shape
    height = eigen_first.shape[0]
    fields = samples * planes
    share = devices // fields
    cols = width // share
    near = [[f * share + c for c in range(share)] for f in range(fields)]
    twins = [
        [(p * samples + s) * share + c for s in range(samples)]
        for p in range(planes)
        for c in range(share)
    ]
    me = lax.axis_index("mode")
    mine = lax.rem(me, share)

    def to_all(blocks):
        return lax.all_to_all(blocks, "mode", split_axis=0, concat_axis=0, tiled=True)

    def to_rows(field):
        return lax.all_to_all(
            field, "mode", split_axis=0, concat_axis=1, axis_index_groups=near, tiled=True
        )

    def to_columns(field):
        return lax.all_to_all(
            field, "mode", split_axis=1, concat_axis=0, axis_index_groups=near, tiled=True
        )

    def give_back(field):
        got = to_all(field.reshape(devices, rows, cols))
        got = got.reshape(planes, samples, share, rows, cols)
        return got.transpose(1, 0, 3, 2, 4).reshape(right_side.shape)

    level = jnp.take(noise_table, 0) * jnp.ones(classes.shape, jnp.float32)
    for index in range(1, noise_table.shape[0]):
        level = jnp.where(classes == index, noise_table[index], level)
    mean_noise = jnp.mean(noise_table)

    part = cols // samples
    outgoing = level.reshape(planes, rows, share, samples, part).transpose(0, 3, 2, 1, 4)
    quarter = to_all(outgoing.reshape(devices, rows, part)).reshape(height, part)
    noise = lax.all_gather(quarter, "mode", axis=1, axis_index_groups=twins, tiled=True)

    all_second = lax.all_gather(eigen_second, "mode", tiled=True)
    weights = 1.0 / (eigen_first[:, None] * all_second[None, :] + mean_noise)
    row_count = height // share
    row_weights = lax.dynamic_slice_in_dim(weights, mine * row_count, row_count, 0)
    col_weights = lax.dynamic_slice_in_dim(weights, mine * cols, cols, 1)

    turned = on_second(basis_second, right_side.reshape(-1, width), True)
    outgoing = turned.reshape(samples, planes, rows, share, cols).transpose(1, 0, 3, 2, 4)
    incoming = to_all(outgoing.reshape(devices, rows, cols)).reshape(height, cols)

    spectrum = on_first(basis_first, incoming, True)
    weighted = col_weights * spectrum
    gamma_part = jnp.sum(spectrum * weighted)
    spectrum_rows = to_rows(spectrum)
    direction_rows = on_second(basis_second, to_rows(on_first(basis_first, weighted)))
    direction = to_columns(direction_rows)
    image = on_first(kernel_first, to_columns(on_second(kernel_second, direction_rows)))
    image = image + noise * direction
    curve_part = jnp.sum(direction * image)
    gamma, curvature = lax.psum(jnp.stack([gamma_part, curve_part]), "mode")
    alpha = gamma / curvature
    change = on_second(basis_second, to_rows(on_first(basis_first, image, True)), True)
    spectrum_rows = spectrum_rows - alpha * change
    weighted = row_weights * spectrum_rows
    gamma_part = jnp.sum(spectrum_rows * weighted)
    later_rows = to_columns(on_second(basis_second, weighted))
    later = on_first(basis_first, later_rows)
    later_image = on_first(kernel_first, to_columns(on_second(kernel_second, to_rows(later))))
    later_image = later_image + noise * later
    parts = jnp.stack([gamma_part, jnp.sum(later * later_image), jnp.sum(later * image)])
    gamma_new, own, cross = lax.psum(parts, "mode")
    ratio = gamma_new / gamma
    step = gamma_new / (own + ratio * (2.0 * cross + ratio * curvature))
    before = alpha + step * ratio
    solution_field = give_back(before * direction + step * later)
    applied = give_back(before * image + step * later_image)
    return solution_field, right_side - applied


LANES = 128
CHUNK = 128
TILE = 256
F32 = jnp.float32
BF16 = jnp.bfloat16


def chip_kernel(
    dims, table, right, classes, tile_two, eig_one, kern_one, kern_two, base_one, base_two,
    sol_out, res_out,
    turned, incoming, level, noise, eig_tiles, eig_row, base_one_t, base_two_t,
    high, low, right_high, right_low, spectrum, spec_rows, dir_rows, dir_cols, image,
    later, work, send, recv, sums, totals, applied_in,
    big_send, big_recv, twin_send, twin_recv, ex_send, ex_recv,
):
    M, S, PL, rows, width, height = dims
    HR, HC = height // 2, width // 2
    part = HC // S
    per = width // M
    line = lax.axis_index("blocks")
    me = lax.axis_index("mode")
    mine = lax.rem(me, 2)
    other = 1 - mine
    field = me // 2
    my_plane, my_sample = field // S, lax.rem(field, S)
    barrier = pltpu.get_barrier_semaphore()

    def device(m):
        return (line, m)

    @pl.loop(1, M)
    def _(d):
        pl.semaphore_signal(barrier, inc=1, device_id=device(lax.rem(me + d, M)), device_id_type=pl.DeviceIdType.MESH)

    def remote(src, dst, sem_send, sem_recv, m):
        return pltpu.make_async_remote_copy(
            src_ref=src, dst_ref=dst, send_sem=sem_send, recv_sem=sem_recv,
            device_id=device(m), device_id_type=pl.DeviceIdType.MESH,
        )

    def place(m):
        f = m // 2
        return f // S, lax.rem(f, S), lax.rem(m, 2)

    def rows_of(index, size, count):
        return pl.ds(pl.multiple_of(index * size, size), count)

    def block(index, size):
        return rows_of(index, size, size)

    def copy_turned(d):
        m = lax.rem(me + d, M)
        p, s, c = place(m)
        return remote(
            turned.at[c, block(s * PL + p, rows)], incoming.at[block(me, rows)],
            big_send.at[0, d], big_recv.at[0, d], m,
        )

    def copy_level(d):
        m = lax.rem(me + d, M)
        p, s, c = place(m)
        return remote(
            level.at[p, :, block(c * S + s, part)], noise.at[s, block(me, rows)],
            big_send.at[1, d], big_recv.at[1, d], m,
        )

    def copy_eig(d):
        m = lax.rem(me + d, M)
        return remote(eig_tiles.at[me], eig_tiles.at[me], big_send.at[2, d], big_recv.at[2, d], m)

    def copy_total(which, d):
        m = lax.rem(me + d, M)
        return remote(
            totals.at[which, me], totals.at[which, me],
            big_send.at[3 + which, d], big_recv.at[3 + which, d], m,
        )

    def copy_sol(d):
        m = lax.rem(me + d, M)
        return remote(
            dir_cols.at[block(m, rows)], sol_out.at[my_sample, my_plane, :, block(mine, HC)],
            big_send.at[5, d], big_recv.at[5, d], m,
        )

    def copy_applied(d):
        m = lax.rem(me + d, M)
        return remote(
            image.at[block(m, rows)], applied_in.at[me],
            big_send.at[6, d], big_recv.at[6, d], m,
        )

    def copy_twin(o):
        s = lax.rem(my_sample + o, S)
        return remote(
            noise.at[my_sample], noise.at[my_sample], twin_send.at[o], twin_recv.at[o],
            (my_plane * S + s) * 2 + mine,
        )

    def copy_near(e, src):
        return remote(src, recv.at[e], ex_send.at[e], ex_recv.at[e], me - mine + other)

    def split_to(hi, lo, value, *index):
        h = value.astype(BF16)
        hi[index] = h
        lo[index] = (value - h.astype(F32)).astype(BF16)

    def mxu(a, b):
        return jnp.dot(a, b, preferred_element_type=F32)

    def chunks(fn):
        @pl.loop(0, HR // CHUNK)
        def _(i):
            fn(pl.multiple_of(i * CHUNK, CHUNK))

    def split_half(k, get):
        def one(i):
            split_to(high, low, get(i), k, pl.ds(i, CHUNK), slice(None))

        chunks(one)

    def product(left, mat, h, ks, out, add=False):
        @pl.loop(0, HC // TILE)
        def _(n):
            lane = pl.multiple_of(n * TILE, TILE)
            total = None
            for k in ks:
                if left:
                    a = mat[block(h, HR), block(k, HR)]
                    term = mxu(a, high[k, :, pl.ds(lane, TILE)]) + mxu(a, low[k, :, pl.ds(lane, TILE)])
                else:
                    b = mat[block(k, HC), pl.ds(pl.multiple_of(h * HC + lane, TILE), TILE)]
                    term = mxu(high[k], b) + mxu(low[k], b)
                total = term if total is None else total + term
            if add:
                total = total + out[:, pl.ds(lane, TILE)]
            out[:, pl.ds(lane, TILE)] = total

    def arrive(e):
        copy_near(e, send.at[0]).wait_recv()
        split_half(other, lambda i: recv[e, pl.ds(i, CHUNK)])

    def both(left, mat, outs, source=None):
        if source is None:
            for h, out in outs:
                product(left, mat, h, (0, 1), out)
        else:
            for h, out in outs:
                product(left, mat, h, (mine,), out)
            arrive(source)
            for h, out in outs:
                product(left, mat, h, (other,), out, True)

    def cross(left, mat, e, slot, own, source=None):
        out = send.at[slot]
        if source is None:
            product(left, mat, other, (0, 1), out)
            copy_near(e, out).start()
            product(left, mat, mine, (0, 1), own)
        else:
            product(left, mat, other, (mine,), out)
            product(left, mat, mine, (mine,), own)
            arrive(source)
            product(left, mat, other, (other,), out, True)
            copy_near(e, out).start()
            product(left, mat, mine, (other,), own, True)
        split_half(mine, lambda i: own[pl.ds(i, CHUNK)])

    def add_sum(index, value):
        sums[index] += jnp.sum(value.reshape(CHUNK // 8, 8, HC), axis=0)

    def start_total(which, count):
        line_index = lax.broadcasted_iota(jnp.int32, (8, LANES), 0)
        tile = jnp.zeros((8, LANES), F32)
        for q in range(count):
            tile = jnp.where(line_index == q, jnp.sum(sums[2 * which + q]), tile)
        totals[which, me] = tile

        @pl.loop(1, M)
        def _(d):
            copy_total(which, d).start()

    def end_total(which):
        @pl.loop(1, M)
        def _(d):
            copy_total(which, d).wait()

        return jnp.sum(totals[which], axis=0)

    sums[...] = jnp.zeros_like(sums)
    count = S * PL * rows

    @pl.loop(0, S)
    def _(s):
        @pl.loop(0, PL)
        def _(p):
            split_to(right_high, right_low, right[s, p], block(s * PL + p, rows), slice(None))

    def turn(c):
        @pl.loop(0, HC // TILE)
        def _(n):
            lane = pl.multiple_of(n * TILE, TILE)
            b = base_two[:, pl.ds(pl.multiple_of(c * HC + lane, TILE), TILE)]
            turned[c, :, pl.ds(lane, TILE)] = mxu(right_high[...], b) + mxu(right_low[...], b)

    pl.semaphore_wait(barrier, M - 1)
    eig_tiles[me] = tile_two[...]

    @pl.loop(1, M)
    def _(d):
        copy_eig(d).start()

    turn(mine)

    @pl.loop(1, M // 2)
    def _(i):
        copy_turned(2 * i).start()

    turn(other)

    @pl.loop(0, M // 2)
    def _(i):
        copy_turned(2 * i + 1).start()

    incoming[block(me, rows)] = turned[mine, block(my_sample * PL + my_plane, rows)]

    @pl.loop(0, PL)
    def _(p):
        kind = classes[p]
        value = jnp.full(kind.shape, table[0], F32)
        for index in range(1, table.shape[0]):
            value = jnp.where(kind == index, table[index], value)
        level[p] = value

    @pl.loop(1, M)
    def _(d):
        copy_level(d).start()

    noise[my_sample, block(me, rows)] = level[my_plane, :, block(mine * S + my_sample, part)]
    mean_noise = table[0]
    for index in range(1, table.shape[0]):
        mean_noise = mean_noise + table[index]
    mean_noise = mean_noise / table.shape[0]

    for a in range(height // TILE):
        for b in range(height // TILE):
            sa, sb = slice(a * TILE, (a + 1) * TILE), slice(b * TILE, (b + 1) * TILE)
            base_one_t[sa, sb] = base_one[sb, sa].astype(F32).T.astype(BF16)
    for a in range(width // TILE):
        for b in range(width // TILE):
            sa, sb = slice(a * TILE, (a + 1) * TILE), slice(b * TILE, (b + 1) * TILE)
            base_two_t[sa, sb] = base_two[sb, sa].astype(F32).T.astype(BF16)

    @pl.loop(1, M)
    def _(d):
        copy_eig(d).wait()

    fold = LANES // per
    for k in range(width // LANES):
        total = eig_tiles[k * fold]
        for q in range(1, fold):
            total = total + eig_tiles[k * fold + q]
        eig_row[:, k * LANES:(k + 1) * LANES] = total

    def weights(row, half):
        e2 = eig_row[0:1, block(half, HC)]
        return 1.0 / (eig_one[pl.ds(row, CHUNK), :] * e2 + mean_noise)

    @pl.loop(1, M)
    def _(d):
        copy_turned(d).wait()

    for k in range(2):
        split_half(k, lambda i: incoming[pl.ds(k * HR + i, CHUNK)])
    both(True, base_one_t, [(h, spectrum.at[h]) for h in range(2)])
    copy_near(0, spectrum.at[other]).start()
    for h in range(2):
        def weigh(i):
            value = spectrum[h, pl.ds(i, CHUNK)]
            scaled = weights(pl.multiple_of(h * HR + i, CHUNK), mine) * value
            add_sum(0, value * scaled)
            split_to(high, low, scaled, h, pl.ds(i, CHUNK), slice(None))

        chunks(weigh)
    cross(True, base_one, 1, 0, work)
    both(False, base_two_t, [(h, dir_rows.at[h]) for h in range(2)], 1)
    copy_near(2, dir_rows.at[other]).start()
    for h in range(2):
        split_half(h, lambda i: dir_rows[h, pl.ds(i, CHUNK)])
    cross(False, kern_two, 3, 1, work)

    both(True, kern_one, [(h, image.at[pl.ds(h * HR, HR)]) for h in range(2)], 3)

    @pl.loop(1, M)
    def _(d):
        copy_level(d).wait()

    for o in range(1, S):
        copy_twin(o).start()
    copy_near(2, dir_rows.at[other]).wait_recv()
    dir_cols[block(mine, HR)] = dir_rows[mine]
    dir_cols[block(other, HR)] = recv[2]
    for o in range(1, S):
        copy_twin(o).wait()

    def noisy(row, value):
        local = jnp.concatenate([noise[s, pl.ds(row, CHUNK)] for s in range(S)], axis=1)
        return local * value

    for h in range(2):
        def finish(i):
            row = pl.multiple_of(h * HR + i, CHUNK)
            value = dir_cols[pl.ds(row, CHUNK)]
            result = image[pl.ds(row, CHUNK)] + noisy(row, value)
            image[pl.ds(row, CHUNK)] = result
            add_sum(1, value * result)
            split_to(high, low, result, h, pl.ds(i, CHUNK), slice(None))

        chunks(finish)
    start_total(0, 2)
    cross(True, base_one_t, 4, 2, work)
    both(False, base_two, [(h, spec_rows.at[h]) for h in range(2)], 4)
    copy_near(0, spectrum.at[other]).wait_recv()
    first = end_total(0)
    gamma, curvature = first[0:1, 0:1], first[1:2, 0:1]
    alpha = gamma / curvature

    def next_weigh(h, get):
        def one(i):
            value = get(i) - alpha * spec_rows[h, pl.ds(i, CHUNK)]
            scaled = weights(pl.multiple_of(mine * HR + i, CHUNK), h) * value
            add_sum(2, value * scaled)
            split_to(high, low, scaled, h, pl.ds(i, CHUNK), slice(None))

        chunks(one)

    next_weigh(mine, lambda i: spectrum[mine, pl.ds(i, CHUNK)])
    next_weigh(other, lambda i: recv[0, pl.ds(i, CHUNK)])
    cross(False, base_two_t, 5, 3, work)
    both(True, base_one, [(h, later.at[pl.ds(h * HR, HR)]) for h in range(2)], 5)
    copy_near(6, later.at[block(other, HR)]).start()
    split_half(mine, lambda i: later[pl.ds(pl.multiple_of(mine * HR + i, CHUNK), CHUNK)])
    cross(False, kern_two, 7, 4, work, 6)
    both(True, kern_one, [(h, spec_rows.at[h]) for h in range(2)], 7)
    for h in range(2):
        def finish_later(i):
            row = pl.multiple_of(h * HR + i, CHUNK)
            value = later[pl.ds(row, CHUNK)]
            result = spec_rows[h, pl.ds(i, CHUNK)] + noisy(row, value)
            spec_rows[h, pl.ds(i, CHUNK)] = result
            add_sum(3, value * result)
            add_sum(4, value * image[pl.ds(row, CHUNK)])

        chunks(finish_later)
    start_total(1, 3)
    for e, ref in ((0, spectrum.at[other]), (1, send.at[0]), (2, dir_rows.at[other]), (3, send.at[1]),
                   (4, send.at[2]), (5, send.at[3]), (6, later.at[block(other, HR)]), (7, send.at[4])):
        copy_near(e, ref).wait_send()
    second_total = end_total(1)
    gamma_new, own, mixed = second_total[0:1, 0:1], second_total[1:2, 0:1], second_total[2:3, 0:1]
    ratio = gamma_new / gamma
    step = gamma_new / (own + ratio * (2.0 * mixed + ratio * curvature))
    before = alpha + step * ratio

    def combine(m):
        spot = block(m, rows)
        half, inner = m // (M // 2), block(lax.rem(m, M // 2), rows)
        dir_cols[spot] = before * dir_cols[spot] + step * later[spot]
        image[spot] = before * image[spot] + step * spec_rows[half, inner]

    @pl.loop(1, M)
    def _(d):
        combine(lax.rem(me + d, M))
        copy_applied(d).start()
        copy_sol(d).start()

    combine(me)
    sol_out[my_sample, my_plane, :, block(mine, HC)] = dir_cols[block(me, rows)]
    res_out[my_sample, my_plane, :, block(mine, HC)] = (
        right[my_sample, my_plane, :, block(mine, HC)] - image[block(me, rows)]
    )

    @pl.loop(1, M)
    def _(d):
        copy_applied(d).wait()
        source = lax.rem(me + M - d, M)
        p, s, c = place(source)
        spot = block(c, HC)
        res_out[s, p, :, spot] = right[s, p, :, spot] - applied_in[source]

    @pl.loop(1, M)
    def _(d):
        copy_sol(d).wait()


def chip_body(
    right_side, classes, noise_table, kernel_first, kernel_second, basis_first, basis_second,
    eigen_first, eigen_second,
):
    M = lax.axis_size("mode")
    S, PL, rows, width = right_side.shape
    height = eigen_first.shape[0]
    HR, HC = height // 2, width // 2
    per = eigen_second.shape[0]
    fold = LANES // per
    spot = lax.rem(lax.axis_index("mode"), fold)
    lanes = jnp.arange(LANES)
    tile = jnp.where(lanes // per == spot, jnp.tile(eigen_second, fold), 0.0)
    tile = jnp.broadcast_to(tile[None], (8, LANES))
    vmem = pl.BlockSpec(memory_space=pltpu.VMEM)
    smem = pl.BlockSpec(memory_space=pltpu.SMEM)
    V = pltpu.VMEM
    field = jax.ShapeDtypeStruct(right_side.shape, F32)
    halves = V((2, HR, HC), F32)
    whole = V((height, HC), F32)

    def kernel(*refs):
        chip_kernel((M, S, PL, rows, width, height), *refs)

    return pl.pallas_call(
        kernel,
        out_shape=(field, field),
        in_specs=[smem] + [vmem] * 8,
        out_specs=(vmem, vmem),
        scratch_shapes=[
            V((2, S * PL * rows, HC), F32), whole, V((PL, rows, width), F32),
            V((S, height, HC // S), F32), V((M, 8, LANES), F32), V((8, width), F32),
            V((height, height), BF16), V((width, width), BF16),
            V((2, HR, HC), BF16), V((2, HR, HC), BF16),
            V((S * PL * rows, width), BF16), V((S * PL * rows, width), BF16),
            halves, halves, halves, whole, whole, whole, V((HR, HC), F32),
            V((5, HR, HC), F32), V((8, HR, HC), F32), V((5, 8, HC), F32),
            V((2, M, 8, LANES), F32), V((M, rows, HC), F32),
            pltpu.SemaphoreType.DMA((7, M)), pltpu.SemaphoreType.DMA((7, M)),
            pltpu.SemaphoreType.DMA((S,)), pltpu.SemaphoreType.DMA((S,)),
            pltpu.SemaphoreType.DMA((8,)), pltpu.SemaphoreType.DMA((8,)),
        ],
        compiler_params=pltpu.CompilerParams(
            collective_id=0, has_side_effects=True, vmem_limit_bytes=60 * 2**20
        ),
    )(noise_table, right_side, classes, tile, eigen_first.reshape(height, 1),
      kernel_first, kernel_second, basis_first, basis_second)


def body(right_side, classes, noise_table, kernel_first, kernel_second, basis_first, basis_second,
         eigen_first, eigen_second):
    args = (right_side, classes, noise_table, kernel_first, kernel_second, basis_first, basis_second,
            eigen_first, eigen_second)
    M = lax.axis_size("mode")
    S, PL, rows, width = right_side.shape
    height = eigen_first.shape[0]
    fits = (
        M == 2 * S * PL and rows % 16 == 0 and height % (2 * TILE) == 0
        and width % (2 * max(TILE, LANES * S)) == 0 and LANES % eigen_second.shape[0] == 0
        and max(height, width) <= 1024
    )
    return chip_body(*args) if fits else general_body(*args)


def solution(mesh):
    in_specs = (
        P(None, "blocks", "mode", None),
        P("blocks", "mode", None),
        P(),
        P(),
        P(),
        P(),
        P(),
        P(),
        P("mode"),
    )
    out_specs = (P(None, "blocks", "mode", None), P(None, "blocks", "mode", None))
    return jax.shard_map(body, mesh=mesh, in_specs=in_specs, out_specs=out_specs, check_vma=False)
```

```python
import jax
import jax.numpy as jnp
from jax import lax
from jax.experimental import pallas as pl
from jax.experimental.pallas import tpu as pltpu
from jax.sharding import PartitionSpec as P

ITERS = 2


def split(field):
    high = lax.reduce_precision(field, 8, 7)
    return high.astype(jnp.bfloat16), (field - high).astype(jnp.bfloat16)


def dot(left, right, dims):
    return lax.dot_general(left, right, (dims, ((), ())), preferred_element_type=jnp.float32)


def on_first(matrix, field, transposed=False):
    dims = ((0 if transposed else 1,), (0,))
    high, low = split(field)
    return dot(matrix, high, dims) + dot(matrix, low, dims)


def on_second(matrix, field, transposed=False):
    dims = ((1,), (0 if transposed else 1,))
    high, low = split(field)
    return dot(high, matrix, dims) + dot(low, matrix, dims)


def general_body(
    right_side,
    classes,
    noise_table,
    kernel_first,
    kernel_second,
    basis_first,
    basis_second,
    eigen_first,
    eigen_second,
):
    devices = lax.axis_size("mode")
    samples, planes, rows, width = right_side.shape
    height = eigen_first.shape[0]
    fields = samples * planes
    share = devices // fields
    cols = width // share
    near = [[f * share + c for c in range(share)] for f in range(fields)]
    twins = [
        [(p * samples + s) * share + c for s in range(samples)]
        for p in range(planes)
        for c in range(share)
    ]
    me = lax.axis_index("mode")
    mine = lax.rem(me, share)

    def to_all(blocks):
        return lax.all_to_all(blocks, "mode", split_axis=0, concat_axis=0, tiled=True)

    def to_rows(field):
        return lax.all_to_all(
            field, "mode", split_axis=0, concat_axis=1, axis_index_groups=near, tiled=True
        )

    def to_columns(field):
        return lax.all_to_all(
            field, "mode", split_axis=1, concat_axis=0, axis_index_groups=near, tiled=True
        )

    def give_back(field):
        got = to_all(field.reshape(devices, rows, cols))
        got = got.reshape(planes, samples, share, rows, cols)
        return got.transpose(1, 0, 3, 2, 4).reshape(right_side.shape)

    level = jnp.take(noise_table, 0) * jnp.ones(classes.shape, jnp.float32)
    for index in range(1, noise_table.shape[0]):
        level = jnp.where(classes == index, noise_table[index], level)
    mean_noise = jnp.mean(noise_table)

    part = cols // samples
    outgoing = level.reshape(planes, rows, share, samples, part).transpose(0, 3, 2, 1, 4)
    quarter = to_all(outgoing.reshape(devices, rows, part)).reshape(height, part)
    noise = lax.all_gather(quarter, "mode", axis=1, axis_index_groups=twins, tiled=True)

    all_second = lax.all_gather(eigen_second, "mode", tiled=True)
    weights = 1.0 / (eigen_first[:, None] * all_second[None, :] + mean_noise)
    row_count = height // share
    row_weights = lax.dynamic_slice_in_dim(weights, mine * row_count, row_count, 0)
    col_weights = lax.dynamic_slice_in_dim(weights, mine * cols, cols, 1)

    turned = on_second(basis_second, right_side.reshape(-1, width), True)
    outgoing = turned.reshape(samples, planes, rows, share, cols).transpose(1, 0, 3, 2, 4)
    incoming = to_all(outgoing.reshape(devices, rows, cols)).reshape(height, cols)

    spectrum = on_first(basis_first, incoming, True)
    weighted = col_weights * spectrum
    gamma_part = jnp.sum(spectrum * weighted)
    spectrum_rows = to_rows(spectrum)
    direction_rows = on_second(basis_second, to_rows(on_first(basis_first, weighted)))
    direction = to_columns(direction_rows)
    image = on_first(kernel_first, to_columns(on_second(kernel_second, direction_rows)))
    image = image + noise * direction
    curve_part = jnp.sum(direction * image)
    gamma, curvature = lax.psum(jnp.stack([gamma_part, curve_part]), "mode")
    alpha = gamma / curvature
    change = on_second(basis_second, to_rows(on_first(basis_first, image, True)), True)
    spectrum_rows = spectrum_rows - alpha * change
    weighted = row_weights * spectrum_rows
    gamma_part = jnp.sum(spectrum_rows * weighted)
    later_rows = to_columns(on_second(basis_second, weighted))
    later = on_first(basis_first, later_rows)
    later_image = on_first(kernel_first, to_columns(on_second(kernel_second, to_rows(later))))
    later_image = later_image + noise * later
    parts = jnp.stack([gamma_part, jnp.sum(later * later_image), jnp.sum(later * image)])
    gamma_new, own, cross = lax.psum(parts, "mode")
    ratio = gamma_new / gamma
    step = gamma_new / (own + ratio * (2.0 * cross + ratio * curvature))
    before = alpha + step * ratio
    solution_field = give_back(before * direction + step * later)
    applied = give_back(before * image + step * later_image)
    return solution_field, right_side - applied


LANES = 128
CHUNK = 128
TILE = 256
F32 = jnp.float32
BF16 = jnp.bfloat16


def chip_kernel(
    dims, table, right, classes, tile_two, eig_one, kern_one, kern_two, base_one, base_two,
    sol_out, res_out,
    turned, incoming, level, noise, eig_tiles, eig_row, base_one_t, base_two_t,
    high, low, right_high, right_low, spectrum, spec_rows, dir_rows, dir_cols, image,
    later, work, send, recv, sums, totals, applied_in,
    big_send, big_recv, twin_send, twin_recv, ex_send, ex_recv,
):
    M, S, PL, rows, width, height = dims
    HR, HC = height // 2, width // 2
    part = HC // S
    per = width // M
    line = lax.axis_index("blocks")
    me = lax.axis_index("mode")
    mine = lax.rem(me, 2)
    other = 1 - mine
    field = me // 2
    my_plane, my_sample = field // S, lax.rem(field, S)
    barrier = pltpu.get_barrier_semaphore()

    def device(m):
        return (line, m)

    @pl.loop(1, M)
    def _(d):
        pl.semaphore_signal(barrier, inc=1, device_id=device(lax.rem(me + d, M)), device_id_type=pl.DeviceIdType.MESH)

    def remote(src, dst, sem_send, sem_recv, m):
        return pltpu.make_async_remote_copy(
            src_ref=src, dst_ref=dst, send_sem=sem_send, recv_sem=sem_recv,
            device_id=device(m), device_id_type=pl.DeviceIdType.MESH,
        )

    def place(m):
        f = m // 2
        return f // S, lax.rem(f, S), lax.rem(m, 2)

    def rows_of(index, size, count):
        return pl.ds(pl.multiple_of(index * size, size), count)

    def block(index, size):
        return rows_of(index, size, size)

    def copy_turned(d):
        m = lax.rem(me + d, M)
        p, s, c = place(m)
        return remote(
            turned.at[c, block(s * PL + p, rows)], incoming.at[block(me, rows)],
            big_send.at[0, d], big_recv.at[0, d], m,
        )

    def copy_level(d):
        m = lax.rem(me + d, M)
        p, s, c = place(m)
        return remote(
            level.at[p, :, block(c * S + s, part)], noise.at[s, block(me, rows)],
            big_send.at[1, d], big_recv.at[1, d], m,
        )

    def copy_eig(d):
        m = lax.rem(me + d, M)
        return remote(eig_tiles.at[me], eig_tiles.at[me], big_send.at[2, d], big_recv.at[2, d], m)

    def copy_total(which, d):
        m = lax.rem(me + d, M)
        return remote(
            totals.at[which, me], totals.at[which, me],
            big_send.at[3 + which, d], big_recv.at[3 + which, d], m,
        )

    def copy_sol(d):
        m = lax.rem(me + d, M)
        return remote(
            dir_cols.at[block(m, rows)], sol_out.at[my_sample, my_plane, :, block(mine, HC)],
            big_send.at[5, d], big_recv.at[5, d], m,
        )

    def copy_applied(d):
        m = lax.rem(me + d, M)
        return remote(
            image.at[block(m, rows)], applied_in.at[me],
            big_send.at[6, d], big_recv.at[6, d], m,
        )

    def copy_twin(o, d):
        s = lax.rem(my_sample + o, S)
        spot = noise.at[my_sample, block(lax.rem(me + M - d, M), rows)]
        return remote(
            spot, spot, twin_send.at[o, d], twin_recv.at[o, d], (my_plane * S + s) * 2 + mine
        )

    def forward(first, end):
        @pl.loop(first, end)
        def _(d):
            copy_level(d).wait_recv()
            for o in range(1, S):
                copy_twin(o, d).start()

    def copy_near(e, src):
        return remote(src, recv.at[e], ex_send.at[e], ex_recv.at[e], me - mine + other)

    def split_to(hi, lo, value, *index):
        h = value.astype(BF16)
        hi[index] = h
        lo[index] = (value - h.astype(F32)).astype(BF16)

    def mxu(a, b):
        return jnp.dot(a, b, preferred_element_type=F32)

    def chunks(fn):
        @pl.loop(0, HR // CHUNK)
        def _(i):
            fn(pl.multiple_of(i * CHUNK, CHUNK))

    def split_half(k, get):
        def one(i):
            split_to(high, low, get(i), k, pl.ds(i, CHUNK), slice(None))

        chunks(one)

    def product(left, mat, h, ks, out, add=False):
        @pl.loop(0, HC // TILE)
        def _(n):
            lane = pl.multiple_of(n * TILE, TILE)
            total = None
            for k in ks:
                if left:
                    a = mat[block(h, HR), block(k, HR)]
                    term = mxu(a, high[k, :, pl.ds(lane, TILE)]) + mxu(a, low[k, :, pl.ds(lane, TILE)])
                else:
                    b = mat[block(k, HC), pl.ds(pl.multiple_of(h * HC + lane, TILE), TILE)]
                    term = mxu(high[k], b) + mxu(low[k], b)
                total = term if total is None else total + term
            if add:
                total = total + out[:, pl.ds(lane, TILE)]
            out[:, pl.ds(lane, TILE)] = total

    def arrive(e):
        copy_near(e, send.at[0]).wait_recv()
        split_half(other, lambda i: recv[e, pl.ds(i, CHUNK)])

    def both(left, mat, outs, source=None):
        if source is None:
            for h, out in outs:
                product(left, mat, h, (0, 1), out)
        else:
            for h, out in outs:
                product(left, mat, h, (mine,), out)
            arrive(source)
            for h, out in outs:
                product(left, mat, h, (other,), out, True)

    def cross(left, mat, e, slot, own, source=None):
        out = send.at[slot]
        if source is None:
            product(left, mat, other, (0, 1), out)
            copy_near(e, out).start()
            product(left, mat, mine, (0, 1), own)
        else:
            product(left, mat, other, (mine,), out)
            product(left, mat, mine, (mine,), own)
            arrive(source)
            product(left, mat, other, (other,), out, True)
            copy_near(e, out).start()
            product(left, mat, mine, (other,), own, True)
        split_half(mine, lambda i: own[pl.ds(i, CHUNK)])

    def add_sum(index, value):
        sums[index] += jnp.sum(value.reshape(CHUNK // 8, 8, HC), axis=0)

    def start_total(which, count):
        line_index = lax.broadcasted_iota(jnp.int32, (8, LANES), 0)
        tile = jnp.zeros((8, LANES), F32)
        for q in range(count):
            tile = jnp.where(line_index == q, jnp.sum(sums[2 * which + q]), tile)
        totals[which, me] = tile

        @pl.loop(1, M)
        def _(d):
            copy_total(which, d).start()

    def end_total(which):
        @pl.loop(1, M)
        def _(d):
            copy_total(which, d).wait()

        return jnp.sum(totals[which], axis=0)

    sums[...] = jnp.zeros_like(sums)
    count = S * PL * rows

    @pl.loop(0, S)
    def _(s):
        @pl.loop(0, PL)
        def _(p):
            split_to(right_high, right_low, right[s, p], block(s * PL + p, rows), slice(None))

    def turn(c):
        @pl.loop(0, HC // TILE)
        def _(n):
            lane = pl.multiple_of(n * TILE, TILE)
            b = base_two[:, pl.ds(pl.multiple_of(c * HC + lane, TILE), TILE)]
            turned[c, :, pl.ds(lane, TILE)] = mxu(right_high[...], b) + mxu(right_low[...], b)

    pl.semaphore_wait(barrier, M - 1)
    eig_tiles[me] = tile_two[...]

    @pl.loop(1, M)
    def _(d):
        copy_eig(d).start()

    turn(mine)

    @pl.loop(1, M // 2)
    def _(i):
        copy_turned(2 * i).start()

    turn(other)

    @pl.loop(0, M // 2)
    def _(i):
        copy_turned(2 * i + 1).start()

    incoming[block(me, rows)] = turned[mine, block(my_sample * PL + my_plane, rows)]

    @pl.loop(0, PL)
    def _(p):
        kind = classes[p]
        value = jnp.full(kind.shape, table[0], F32)
        for index in range(1, table.shape[0]):
            value = jnp.where(kind == index, table[index], value)
        level[p] = value

    @pl.loop(1, M)
    def _(d):
        copy_level(d).start()

    noise[my_sample, block(me, rows)] = level[my_plane, :, block(mine * S + my_sample, part)]
    for o in range(1, S):
        copy_twin(o, 0).start()
    mean_noise = table[0]
    for index in range(1, table.shape[0]):
        mean_noise = mean_noise + table[index]
    mean_noise = mean_noise / table.shape[0]

    for a in range(height // TILE):
        for b in range(height // TILE):
            sa, sb = slice(a * TILE, (a + 1) * TILE), slice(b * TILE, (b + 1) * TILE)
            base_one_t[sa, sb] = base_one[sb, sa].astype(F32).T.astype(BF16)
    for a in range(width // TILE):
        for b in range(width // TILE):
            sa, sb = slice(a * TILE, (a + 1) * TILE), slice(b * TILE, (b + 1) * TILE)
            base_two_t[sa, sb] = base_two[sb, sa].astype(F32).T.astype(BF16)

    @pl.loop(1, M)
    def _(d):
        copy_eig(d).wait()

    fold = LANES // per
    for k in range(width // LANES):
        total = eig_tiles[k * fold]
        for q in range(1, fold):
            total = total + eig_tiles[k * fold + q]
        eig_row[:, k * LANES:(k + 1) * LANES] = total

    def weights(row, half):
        e2 = eig_row[0:1, block(half, HC)]
        return 1.0 / (eig_one[pl.ds(row, CHUNK), :] * e2 + mean_noise)

    @pl.loop(1, M)
    def _(d):
        copy_turned(d).wait()

    for k in range(2):
        split_half(k, lambda i: incoming[pl.ds(k * HR + i, CHUNK)])
    both(True, base_one_t, [(h, spectrum.at[h]) for h in range(2)])
    copy_near(0, spectrum.at[other]).start()
    for h in range(2):
        def weigh(i):
            value = spectrum[h, pl.ds(i, CHUNK)]
            scaled = weights(pl.multiple_of(h * HR + i, CHUNK), mine) * value
            add_sum(0, value * scaled)
            split_to(high, low, scaled, h, pl.ds(i, CHUNK), slice(None))

        chunks(weigh)
    forward(1, 1 + M // 3)
    cross(True, base_one, 1, 0, work)
    both(False, base_two_t, [(h, dir_rows.at[h]) for h in range(2)], 1)
    copy_near(2, dir_rows.at[other]).start()
    for h in range(2):
        split_half(h, lambda i: dir_rows[h, pl.ds(i, CHUNK)])
    forward(1 + M // 3, 1 + 2 * (M // 3))
    cross(False, kern_two, 3, 1, work)

    both(True, kern_one, [(h, image.at[pl.ds(h * HR, HR)]) for h in range(2)], 3)

    forward(1 + 2 * (M // 3), M)
    copy_near(2, dir_rows.at[other]).wait_recv()
    dir_cols[block(mine, HR)] = dir_rows[mine]
    dir_cols[block(other, HR)] = recv[2]

    @pl.loop(0, M)
    def _(d):
        for o in range(1, S):
            copy_twin(o, d).wait()

    @pl.loop(1, M)
    def _(d):
        copy_level(d).wait_send()

    def noisy(row, value):
        local = jnp.concatenate([noise[s, pl.ds(row, CHUNK)] for s in range(S)], axis=1)
        return local * value

    for h in range(2):
        def finish(i):
            row = pl.multiple_of(h * HR + i, CHUNK)
            value = dir_cols[pl.ds(row, CHUNK)]
            result = image[pl.ds(row, CHUNK)] + noisy(row, value)
            image[pl.ds(row, CHUNK)] = result
            add_sum(1, value * result)
            split_to(high, low, result, h, pl.ds(i, CHUNK), slice(None))

        chunks(finish)
    start_total(0, 2)
    cross(True, base_one_t, 4, 2, work)
    both(False, base_two, [(h, spec_rows.at[h]) for h in range(2)], 4)
    copy_near(0, spectrum.at[other]).wait_recv()
    first = end_total(0)
    gamma, curvature = first[0:1, 0:1], first[1:2, 0:1]
    alpha = gamma / curvature

    def next_weigh(h, get):
        def one(i):
            value = get(i) - alpha * spec_rows[h, pl.ds(i, CHUNK)]
            scaled = weights(pl.multiple_of(mine * HR + i, CHUNK), h) * value
            add_sum(2, value * scaled)
            split_to(high, low, scaled, h, pl.ds(i, CHUNK), slice(None))

        chunks(one)

    next_weigh(mine, lambda i: spectrum[mine, pl.ds(i, CHUNK)])
    next_weigh(other, lambda i: recv[0, pl.ds(i, CHUNK)])
    cross(False, base_two_t, 5, 3, work)
    both(True, base_one, [(h, later.at[pl.ds(h * HR, HR)]) for h in range(2)], 5)
    copy_near(6, later.at[block(other, HR)]).start()
    split_half(mine, lambda i: later[pl.ds(pl.multiple_of(mine * HR + i, CHUNK), CHUNK)])
    cross(False, kern_two, 7, 4, work, 6)
    both(True, kern_one, [(h, spec_rows.at[h]) for h in range(2)], 7)
    for h in range(2):
        def finish_later(i):
            row = pl.multiple_of(h * HR + i, CHUNK)
            value = later[pl.ds(row, CHUNK)]
            result = spec_rows[h, pl.ds(i, CHUNK)] + noisy(row, value)
            spec_rows[h, pl.ds(i, CHUNK)] = result
            add_sum(3, value * result)
            add_sum(4, value * image[pl.ds(row, CHUNK)])

        chunks(finish_later)
    start_total(1, 3)
    for e, ref in ((0, spectrum.at[other]), (1, send.at[0]), (2, dir_rows.at[other]), (3, send.at[1]),
                   (4, send.at[2]), (5, send.at[3]), (6, later.at[block(other, HR)]), (7, send.at[4])):
        copy_near(e, ref).wait_send()
    second_total = end_total(1)
    gamma_new, own, mixed = second_total[0:1, 0:1], second_total[1:2, 0:1], second_total[2:3, 0:1]
    ratio = gamma_new / gamma
    step = gamma_new / (own + ratio * (2.0 * mixed + ratio * curvature))
    before = alpha + step * ratio

    def combine(m):
        spot = block(m, rows)
        half, inner = m // (M // 2), block(lax.rem(m, M // 2), rows)
        dir_cols[spot] = before * dir_cols[spot] + step * later[spot]
        image[spot] = before * image[spot] + step * spec_rows[half, inner]

    @pl.loop(1, M)
    def _(d):
        combine(lax.rem(me + d, M))
        copy_applied(d).start()
        copy_sol(d).start()

    combine(me)
    sol_out[my_sample, my_plane, :, block(mine, HC)] = dir_cols[block(me, rows)]
    res_out[my_sample, my_plane, :, block(mine, HC)] = (
        right[my_sample, my_plane, :, block(mine, HC)] - image[block(me, rows)]
    )

    @pl.loop(1, M)
    def _(d):
        copy_applied(d).wait()
        source = lax.rem(me + M - d, M)
        p, s, c = place(source)
        spot = block(c, HC)
        res_out[s, p, :, spot] = right[s, p, :, spot] - applied_in[source]

    @pl.loop(1, M)
    def _(d):
        copy_sol(d).wait()


def chip_body(
    right_side, classes, noise_table, kernel_first, kernel_second, basis_first, basis_second,
    eigen_first, eigen_second,
):
    M = lax.axis_size("mode")
    S, PL, rows, width = right_side.shape
    height = eigen_first.shape[0]
    HR, HC = height // 2, width // 2
    per = eigen_second.shape[0]
    fold = LANES // per
    spot = lax.rem(lax.axis_index("mode"), fold)
    lanes = jnp.arange(LANES)
    tile = jnp.where(lanes // per == spot, jnp.tile(eigen_second, fold), 0.0)
    tile = jnp.broadcast_to(tile[None], (8, LANES))
    vmem = pl.BlockSpec(memory_space=pltpu.VMEM)
    smem = pl.BlockSpec(memory_space=pltpu.SMEM)
    V = pltpu.VMEM
    field = jax.ShapeDtypeStruct(right_side.shape, F32)
    halves = V((2, HR, HC), F32)
    whole = V((height, HC), F32)

    def kernel(*refs):
        chip_kernel((M, S, PL, rows, width, height), *refs)

    return pl.pallas_call(
        kernel,
        out_shape=(field, field),
        in_specs=[smem] + [vmem] * 8,
        out_specs=(vmem, vmem),
        scratch_shapes=[
            V((2, S * PL * rows, HC), F32), whole, V((PL, rows, width), F32),
            V((S, height, HC // S), F32), V((M, 8, LANES), F32), V((8, width), F32),
            V((height, height), BF16), V((width, width), BF16),
            V((2, HR, HC), BF16), V((2, HR, HC), BF16),
            V((S * PL * rows, width), BF16), V((S * PL * rows, width), BF16),
            halves, halves, halves, whole, whole, whole, V((HR, HC), F32),
            V((5, HR, HC), F32), V((8, HR, HC), F32), V((5, 8, HC), F32),
            V((2, M, 8, LANES), F32), V((M, rows, HC), F32),
            pltpu.SemaphoreType.DMA((7, M)), pltpu.SemaphoreType.DMA((7, M)),
            pltpu.SemaphoreType.DMA((S, M)), pltpu.SemaphoreType.DMA((S, M)),
            pltpu.SemaphoreType.DMA((8,)), pltpu.SemaphoreType.DMA((8,)),
        ],
        compiler_params=pltpu.CompilerParams(
            collective_id=0, has_side_effects=True, vmem_limit_bytes=60 * 2**20
        ),
    )(noise_table, right_side, classes, tile, eigen_first.reshape(height, 1),
      kernel_first, kernel_second, basis_first, basis_second)


def body(right_side, classes, noise_table, kernel_first, kernel_second, basis_first, basis_second,
         eigen_first, eigen_second):
    args = (right_side, classes, noise_table, kernel_first, kernel_second, basis_first, basis_second,
            eigen_first, eigen_second)
    M = lax.axis_size("mode")
    S, PL, rows, width = right_side.shape
    height = eigen_first.shape[0]
    fits = (
        M == 2 * S * PL and rows % 16 == 0 and height % (2 * TILE) == 0
        and width % (2 * max(TILE, LANES * S)) == 0 and LANES % eigen_second.shape[0] == 0
        and max(height, width) <= 1024
    )
    return chip_body(*args) if fits else general_body(*args)


def solution(mesh):
    in_specs = (
        P(None, "blocks", "mode", None),
        P("blocks", "mode", None),
        P(),
        P(),
        P(),
        P(),
        P(),
        P(),
        P("mode"),
    )
    out_specs = (P(None, "blocks", "mode", None), P(None, "blocks", "mode", None))
    return jax.shard_map(body, mesh=mesh, in_specs=in_specs, out_specs=out_specs, check_vma=False)
```
